32 devices in a mesh: gx: 8 (over z, x), gy: 4 (over y, core).
Axes of the slice: x: 2, y: 2, z: 4, core: 2. Of those that a mesh axis runs over, the one named last changes fastest.
Arguments:
- tokens: bfloat16 [512, 4096], P('gy', 'gx'), may hold values from -6 to 6
- attn_gain: bfloat16 [4096], replicated, may hold values from 0.099609375 to 1.8984375
- qkv_weight: bfloat16 [4096, 6144], P('gy', 'gx'), may hold values from -0.1875 to 0.1875
- out_weight: bfloat16 [4096, 4096], P('gx', 'gy'), may hold values from -0.09375 to 0.09375
- mlp_gain: bfloat16 [4096], replicated, may hold values from 0.099609375 to 1.8984375
- up_weight: bfloat16 [4096, 12288], P('gy', 'gx'), may hold values from -0.09375 to 0.09375
- down_weight: bfloat16 [12288, 4096], P('gx', 'gy'), may hold values from -0.0546875 to 0.0546875
- final_gain: bfloat16 [4096], replicated, may hold values from 0.099609375 to 1.8984375
- head_weight: bfloat16 [4096, 131072], P(None, ('gx', 'gy')), may hold values from -0.25 to 0.25
- kv_cache: bfloat16 [32, 4096, 256], P(('gy', 'gx')), may hold values from -40 to 40
- cache_lengths: int32 [4], replicated, may hold values from 1 to 3968, as said below
- slot_request: int32 [4], replicated, may hold values from 0 to 3, each once
Outputs:
- hidden_out: bfloat16 [512, 4096], P('gy', 'gx')
- new_cache: bfloat16 [32, 4096, 256], P(('gy', 'gx'))
- last_norms: float32 [4], replicated
- max_logits: float32 [4], replicated
- head_input: bfloat16 [4, 4096], replicated
The draws below stay inside these ranges and needn't reach their ends.
Inputs may be any that keep to these rules, and one draw needn't show every extreme that they name: `cache_lengths`: the longest request has exactly 3968 cached positions.
All inputs are finite; a program needn't handle non-finite values.
Results may differ from the reference program's by a relative error of at most 0.02.
The reference program's roundings to bfloat16 on the way (of `normed`, `qkv_order`, `projected`, `attended`, `middle`, `mlp_input` and `activation`) count: a program that leaves them out, or rounds other values in their place, can miss the bound.
Values may be sent and summed in bfloat16 or wider, within the bound.
No kernel may reach another device: no remote copies, remote signals or barrier semaphores. Data moves between devices by JAX's collectives and lax.ppermute only.
A program may use at most 128 MiB of HBM per device.

```python
import math
import jax
import jax.numpy as jnp
from jax import lax

D = 4096
HEADS = 32
KVH = 8
HD = 128
VOCAB = 131072
FF = 12288
CACHE = 4096
NEW = 128
COPIES = 1
SLOTS = 4
TOKENS = 512
ATT = 4096
QKV = 6144


def draw_kv_cache(key, part):
    key_one = jax.random.fold_in(key, 0)
    values = 2.0 * jax.random.normal(key_one, (SLOTS * KVH, CACHE, 2 * HD), jnp.float32)
    return jnp.clip(values, -40.0, 40.0).astype(jnp.bfloat16)


def draw_cache_lengths(key, part):
    key_one, key_two, key_three = jax.random.split(key, 3)
    longest = CACHE - NEW
    first_draw = jax.random.randint(key_one, (SLOTS,), 1, longest + 1)
    second_draw = jax.random.randint(key_two, (SLOTS,), 1, longest + 1)
    skewed = jnp.maximum(first_draw * second_draw // longest, 1)
    chosen = jax.random.randint(key_three, (), 0, SLOTS)
    return jnp.where(jnp.arange(SLOTS) == chosen, longest, skewed).astype(jnp.int32)


def shard_levels(key, shape, cuts, least, largest):
    level, own = 1.0, jax.random.fold_in(key, 6)
    for axis_at, blocks in cuts:
        draws = jnp.exp(jax.random.uniform(jax.random.fold_in(own, axis_at), (blocks,), jnp.float32, least / len(cuts), largest / len(cuts)))
        level = level * jnp.repeat(draws, shape[axis_at] // blocks).reshape([-1 if axis == axis_at else 1 for axis in range(len(shape))])
    return level


def bell_draw(stream_key, shape, scale, limit, pieces=(), dtype=jnp.bfloat16):
    values = scale * jax.random.normal(stream_key, shape, jnp.float32)
    if pieces:
        values = values * shard_levels(stream_key, shape, pieces, -0.22, 0.18)
    return jnp.clip(values, -limit, limit).astype(dtype)


def setup_inputs(seed: int = 0) -> dict:
    key_list = jax.random.split(jax.random.key(seed), 13)
    return {
        "tokens": bell_draw(key_list[0], (TOKENS, D), 1.0, 6.0, ((0, 4), (1, 8))),
        "attn_gain": jnp.clip(1.0 + 0.18 * jax.random.normal(key_list[1], (D,), jnp.float32), 0.099609375, 1.8984375).astype(jnp.bfloat16),
        "qkv_weight": bell_draw(key_list[2], (D, QKV), (D // 4) ** -0.5, 0.1875, ((0, 4), (1, 8))),
        "out_weight": bell_draw(key_list[3], (ATT, D), ATT ** -0.5, 0.09375, ((0, 8), (1, 4))),
        "mlp_gain": jnp.clip(1.0 + 0.18 * jax.random.normal(key_list[4], (D,), jnp.float32), 0.099609375, 1.8984375).astype(jnp.bfloat16),
        "up_weight": bell_draw(key_list[5], (D, FF), D ** -0.5, 0.09375, ((0, 4), (1, 8))),
        "down_weight": bell_draw(key_list[6], (FF, D), FF ** -0.5, 0.0546875, ((0, 8), (1, 4))),
        "final_gain": jnp.clip(1.0 + 0.18 * jax.random.normal(key_list[7], (D,), jnp.float32), 0.099609375, 1.8984375).astype(jnp.bfloat16),
        "head_weight": bell_draw(key_list[8], (D, VOCAB), (D // 9) ** -0.5, 0.25, ((1, 32),)),
        "kv_cache": draw_kv_cache(jax.random.fold_in(key_list[12], 71), 0),
        "cache_lengths": draw_cache_lengths(jax.random.fold_in(key_list[12], 71), 0),
        "slot_request": jax.random.permutation(key_list[11], SLOTS).astype(jnp.int32),
    }


epsilon = 1e-05

def rms_factor(row_block):
    return lax.rsqrt(lax.optimization_barrier(jnp.mean(row_block * row_block, axis=-1, keepdims=True)) + epsilon)

def reference(tokens, attn_gain, qkv_weight, out_weight, mlp_gain, up_weight, down_weight, final_gain, head_weight, kv_cache, cache_lengths, slot_request):
    per_group = HEADS // KVH
    group_width = (per_group + 2) * HD
    qkv_piece = group_width // COPIES
    out_piece = per_group * HD // COPIES
    qkv_order = qkv_weight.reshape(D, COPIES, KVH, qkv_piece).transpose(0, 2, 1, 3).reshape(D, KVH * group_width)
    out_order = out_weight.reshape(COPIES, KVH, out_piece, D).transpose(1, 0, 2, 3).reshape(ATT, D)
    inputs_f32 = tokens.astype(jnp.float32)
    normed = (inputs_f32 * rms_factor(inputs_f32) * attn_gain.astype(jnp.float32)).astype(jnp.bfloat16)
    projected = jnp.dot(normed, qkv_order, preferred_element_type=jnp.float32).astype(jnp.bfloat16)
    per_slot = projected.reshape(SLOTS, NEW, KVH, group_width).transpose(0, 2, 1, 3).reshape(SLOTS * KVH, NEW, group_width)
    slot_lengths = jnp.repeat(cache_lengths[slot_request], KVH)
    scaling = 1.0 / math.sqrt(HD)
    query_token = jnp.arange(per_group * NEW) % NEW
    causal = jnp.arange(NEW)[None, :] <= query_token[:, None]
    cache_pos = jnp.arange(CACHE)

    def attend(item_parts):
        group_cols, cache_rows, length = item_parts
        queries = group_cols[:, :per_group * HD].reshape(NEW, per_group, HD).transpose(1, 0, 2).reshape(per_group * NEW, HD)
        key_new = group_cols[:, per_group * HD:(per_group + 1) * HD]
        value_new = group_cols[:, (per_group + 1) * HD:]
        cache_scores = jnp.dot(queries, cache_rows[:, :HD].T, preferred_element_type=jnp.float32) * scaling
        cache_scores = jnp.where(cache_pos[None, :] < length, cache_scores, -jnp.inf)
        new_scores = jnp.dot(queries, key_new.T, preferred_element_type=jnp.float32) * scaling
        new_scores = jnp.where(causal, new_scores, -jnp.inf)
        row_max = jnp.maximum(lax.optimization_barrier(jnp.max(cache_scores, axis=1, keepdims=True)), lax.optimization_barrier(jnp.max(new_scores, axis=1, keepdims=True)))
        cache_weights = jnp.exp(cache_scores - row_max)
        new_weights = jnp.exp(new_scores - row_max)
        denominator = lax.optimization_barrier(jnp.sum(cache_weights, axis=1, keepdims=True)) + lax.optimization_barrier(jnp.sum(new_weights, axis=1, keepdims=True))
        numerator = jnp.dot(cache_weights.astype(jnp.bfloat16), cache_rows[:, HD:], preferred_element_type=jnp.float32)
        numerator = numerator + jnp.dot(new_weights.astype(jnp.bfloat16), value_new, preferred_element_type=jnp.float32)
        attended = (numerator / denominator).astype(jnp.bfloat16)
        attended = attended.reshape(per_group, NEW, HD).transpose(1, 0, 2).reshape(NEW, per_group * HD)
        fresh = jnp.concatenate([key_new, value_new], axis=1)
        appended = lax.dynamic_update_slice(cache_rows, fresh, (length.astype(jnp.int32), jnp.zeros((), jnp.int32)))
        return (attended, appended)
    attended, new_cache = lax.map(attend, (per_slot, kv_cache, slot_lengths))
    attention = attended.reshape(SLOTS, KVH, NEW, per_group * HD).transpose(0, 2, 1, 3).reshape(TOKENS, ATT)
    middle_f32 = inputs_f32 + jnp.dot(attention, out_order, preferred_element_type=jnp.float32)
    middle = lax.optimization_barrier(middle_f32.astype(jnp.bfloat16))
    middle_in = middle.astype(jnp.float32)
    mlp_input = (middle_in * rms_factor(middle_in) * mlp_gain.astype(jnp.float32)).astype(jnp.bfloat16)
    up_values = jnp.dot(mlp_input, up_weight, preferred_element_type=jnp.float32)
    rectified = jnp.maximum(up_values, 0.0)
    activation = (rectified * rectified).astype(jnp.bfloat16)
    hidden_out = (middle_in + jnp.dot(activation, down_weight, preferred_element_type=jnp.float32)).astype(jnp.bfloat16)
    final_rows = hidden_out.reshape(SLOTS, NEW, D)[:, NEW - 1, :].astype(jnp.float32)
    mean_square = lax.optimization_barrier(jnp.mean(final_rows * final_rows, axis=1))
    last_norms = jnp.sqrt(mean_square)
    head_input = (final_rows * lax.rsqrt(mean_square + epsilon)[:, None] * final_gain.astype(jnp.float32)).astype(jnp.bfloat16)
    logits = jnp.dot(head_input, head_weight, preferred_element_type=jnp.float32)
    max_logits = lax.optimization_barrier(jnp.max(logits, axis=1))
    return (hidden_out, new_cache, last_norms, max_logits, head_input)
```

```python
import math

import jax
import jax.numpy as jnp
from jax import lax
from jax.experimental import pallas as pl
from jax.experimental.pallas import tpu as pltpu
from jax.sharding import PartitionSpec as P

HEADS = 32
KVH = 8
HD = 128


epsilon = 1e-05
negative = -1e30


def from_partner(block, axis, distance):
    count = lax.axis_size(axis)
    route = []
    for low in range(count):
        high = low | 1 << distance
        if high != low and high < count:
            route += [(low, high), (high, low)]
    return lax.ppermute(block, axis, route)


def rms_factor(row_block):
    return lax.rsqrt(jnp.mean(row_block * row_block, axis=-1, keepdims=True) + epsilon)


def gather_features(shard_rows):
    return lax.all_gather(shard_rows, "gx", axis=1, tiled=True)


def rows_product(left_rows, weight_shard):
    return jnp.dot(
        left_rows,
        lax.all_gather(weight_shard, "gy", axis=0, tiled=True),
        preferred_element_type=jnp.float32,
    )


def columns_product(left_rows, weight_shard):
    return jnp.dot(
        left_rows,
        lax.all_gather(weight_shard, "gy", axis=1, tiled=True),
        preferred_element_type=jnp.float32,
    )


def pair_swap(values):
    return from_partner(values, "gx", KVH.bit_length() - 1)


def scatter_partials(partial_terms):
    return lax.psum_scatter(
        partial_terms.astype(jnp.bfloat16), "gx", scatter_dimension=1, tiled=True
    ).astype(jnp.float32)


def merge_block(carried, scores, value_rows):
    row_max, running, numerator = carried
    new_max = jnp.maximum(row_max, jnp.max(scores, axis=1, keepdims=True))
    factor = jnp.exp(row_max - new_max)
    weights = jnp.exp(scores - new_max)
    running = running * factor + jnp.sum(weights, axis=1, keepdims=True)
    numerator = numerator * factor + jnp.dot(
        weights.astype(jnp.bfloat16), value_rows, preferred_element_type=jnp.float32
    )
    return (new_max, running, numerator)


def attend_cache(group_cols, cache_rows, length, new_rows):
    per_group = HEADS // KVH
    scaling = 1.0 / math.sqrt(HD)
    query_rows = per_group * new_rows
    queries = (
        group_cols[:, : per_group * HD]
        .reshape(new_rows, per_group, HD)
        .transpose(1, 0, 2)
        .reshape(query_rows, HD)
    )
    key_new = group_cols[:, per_group * HD : (per_group + 1) * HD]
    value_new = group_cols[:, (per_group + 1) * HD :]
    block_len = min(512, cache_rows.shape[0])

    def visit_block(step_index, carried):
        offset = step_index * block_len
        block_rows = lax.dynamic_slice_in_dim(cache_rows, offset, block_len, 0)
        scores = (
            jnp.dot(queries, block_rows[:, :HD].T, preferred_element_type=jnp.float32) * scaling
        )
        positions = offset + jnp.arange(block_len)
        scores = jnp.where(positions[None, :] < length, scores, negative)
        return merge_block(carried, scores, block_rows[:, HD:])

    initial = (
        jnp.full((query_rows, 1), negative, jnp.float32),
        jnp.zeros((query_rows, 1), jnp.float32),
        jnp.zeros((query_rows, HD), jnp.float32),
    )
    block_count = (length + block_len - 1) // block_len
    carried = lax.fori_loop(0, block_count, visit_block, initial)
    new_scores = jnp.dot(queries, key_new.T, preferred_element_type=jnp.float32) * scaling
    causal = jnp.arange(new_rows)[None, :] <= (jnp.arange(query_rows) % new_rows)[:, None]
    new_scores = jnp.where(causal, new_scores, negative)
    row_max, running, numerator = merge_block(carried, new_scores, value_new)
    attended = (numerator / running).astype(jnp.bfloat16)
    attended = (
        attended.reshape(per_group, new_rows, HD)
        .transpose(1, 0, 2)
        .reshape(new_rows, per_group * HD)
    )
    fresh = jnp.concatenate([key_new, value_new], axis=1)
    appended = lax.dynamic_update_slice(cache_rows, fresh, (length, jnp.zeros((), jnp.int32)))
    return (attended, appended)


def local(
    tokens,
    attn_gain,
    qkv_weight,
    out_weight,
    mlp_gain,
    up_weight,
    down_weight,
    final_gain,
    head_weight,
    kv_cache,
    cache_lengths,
    slot_request,
):
    gx_count = lax.axis_size("gx")
    gy_count = lax.axis_size("gy")
    copies = gx_count // KVH
    gx_place = lax.axis_index("gx")
    copy_index = gx_place // KVH
    slot_index = lax.axis_index("gy") * copies + copy_index
    new_rows = tokens.shape[0] // copies
    feature_cols = tokens.shape[1]
    gathered_tokens = gather_features(tokens)
    tokens_f32 = gathered_tokens.astype(jnp.float32)
    normed = (tokens_f32 * rms_factor(tokens_f32) * attn_gain.astype(jnp.float32)).astype(
        jnp.bfloat16
    )
    projected = rows_product(normed, qkv_weight).astype(jnp.bfloat16)
    if copies == 2:
        own_half = lax.dynamic_slice_in_dim(projected, copy_index * new_rows, new_rows, 0)
        sent_rows = lax.dynamic_slice_in_dim(projected, (1 - copy_index) * new_rows, new_rows, 0)
        received = pair_swap(sent_rows)
        group_cols = jnp.where(
            copy_index == 0,
            jnp.concatenate([own_half, received], axis=1),
            jnp.concatenate([received, own_half], axis=1),
        )
    else:
        group_cols = projected
    length = cache_lengths[slot_request[slot_index]]
    attended, appended = attend_cache(group_cols, kv_cache[0], length, new_rows)
    new_cache = appended[None]
    if copies == 2:
        half_width = attended.shape[1] // 2
        kept_half = lax.dynamic_slice_in_dim(attended, copy_index * half_width, half_width, 1)
        handed = lax.dynamic_slice_in_dim(attended, (1 - copy_index) * half_width, half_width, 1)
        returned = pair_swap(handed)
        attention_rows = jnp.where(
            copy_index == 0,
            jnp.concatenate([kept_half, returned], axis=0),
            jnp.concatenate([returned, kept_half], axis=0),
        )
    else:
        attention_rows = attended
    attention_terms = columns_product(attention_rows, out_weight)
    middle = (tokens.astype(jnp.float32) + scatter_partials(attention_terms)).astype(jnp.bfloat16)
    middle_full = gather_features(middle)
    middle_f32 = middle_full.astype(jnp.float32)
    mlp_input = (middle_f32 * rms_factor(middle_f32) * mlp_gain.astype(jnp.float32)).astype(
        jnp.bfloat16
    )
    up_values = rows_product(mlp_input, up_weight)
    rectified = jnp.maximum(up_values, 0.0)
    activation = (rectified * rectified).astype(jnp.bfloat16)
    down_terms = columns_product(activation, down_weight)
    hidden_out = (middle.astype(jnp.float32) + scatter_partials(down_terms)).astype(jnp.bfloat16)
    final_rows = hidden_out.reshape(copies, new_rows, feature_cols)[:, new_rows - 1, :]
    every_last = lax.all_gather(final_rows, ("gx", "gy"), axis=0, tiled=True)
    slot_rows = every_last.reshape(gx_count, gy_count, copies, feature_cols).transpose(1, 2, 0, 3)
    slot_rows = slot_rows.reshape(gy_count * copies, gx_count * feature_cols).astype(jnp.float32)
    mean_square = jnp.mean(slot_rows * slot_rows, axis=1)
    last_norms = jnp.sqrt(mean_square)
    head_input = (
        slot_rows * lax.rsqrt(mean_square + epsilon)[:, None] * final_gain.astype(jnp.float32)
    ).astype(jnp.bfloat16)
    logits = jnp.dot(head_input, head_weight, preferred_element_type=jnp.float32)
    max_logits = lax.pmax(jnp.max(logits, axis=1), ("gx", "gy"))
    return (hidden_out, new_cache, last_norms, max_logits, head_input)


def xor_permute(values, axis, distance):
    count = lax.axis_size(axis)
    return lax.ppermute(values, axis, [(place, place ^ distance) for place in range(count)])


def transpose_places(block):
    gx_count, gy_count = lax.axis_size("gx"), lax.axis_size("gy")
    halves = gx_count // gy_count
    route = []
    for gx_at in range(gx_count):
        for gy_at in range(gy_count):
            target = (gy_at * halves + gx_at % halves) * gy_count + gx_at // halves
            route.append((gx_at * gy_count + gy_at, target))
    return lax.ppermute(block, ("gx", "gy"), route)


def exchange(blocks, axes):
    return lax.all_to_all(blocks, axes, split_axis=0, concat_axis=0, tiled=True)


def across(block, places):
    return xor_permute(block, "gx", places)


PAIRS = tuple((far, near) for far in range(4) for near in range(2))


def gather_blocks(block):
    found = {(0, 0): block, (0, 1): across(block, 1)}
    for far in (1, 2, 3):
        found[far, 0] = across(block, 2 * far)
    for far in (1, 2, 3):
        found[far, 1] = across(found[far, 0], 1)
    return [found[at] for at in PAIRS]


def scatter_blocks(blocks, tie=None):
    held = dict(zip(PAIRS, blocks))

    def wide(values):
        return values.astype(jnp.float32)

    pairs = [wide(held[far, 0]) + wide(across(held[far, 1], 1)) for far in (2, 3)]
    pairs = [pair.astype(jnp.bfloat16) for pair in pairs]
    if tie is not None:
        *pairs, _ = lax.optimization_barrier((*pairs, tie))
    summed = [across(pair, 2 * far) for far, pair in zip((2, 3), pairs)]
    near = wide(across(held[1, 0], 2)) + wide(across(held[1, 1], 3))
    near = near + wide(held[0, 0]) + wide(across(held[0, 1], 1))
    return near + wide(summed[0]) + wide(summed[1])


def rows_dot(left, weight):
    return lax.dot_general(
        left, weight, (((left.ndim - 1,), (0,)), ((), ())), preferred_element_type=jnp.float32
    )


def attend_kernel(
    place_ref,
    lengths_ref,
    requests_ref,
    group_ref,
    cache_ref,
    out_ref,
    appended_ref,
    rows_ref,
    window_ref,
    numer_ref,
    max_ref,
    sum_ref,
    load_sems,
    copy_sem,
    window_sem,
):
    per_group = HEADS // KVH
    new_rows = group_ref.shape[0]
    query_rows = per_group * new_rows
    block_len = rows_ref.shape[1]
    block_count = rows_ref.shape[0]
    scaling = math.log2(math.e) / math.sqrt(HD)
    length = lengths_ref[requests_ref[place_ref[0]]]

    def load(step):
        source = cache_ref.at[pl.ds(pl.multiple_of(step * block_len, block_len), block_len)]
        return pltpu.make_async_copy(source, rows_ref.at[step], load_sems.at[step])

    for step in range(block_count):
        load(step).start()
    whole_copy = pltpu.make_async_copy(cache_ref, appended_ref, copy_sem)
    whole_copy.start()
    queries = jnp.concatenate(
        [group_ref[:, head * HD : (head + 1) * HD] for head in range(per_group)], axis=0
    )
    key_new = group_ref[:, per_group * HD : (per_group + 1) * HD]
    value_new = group_ref[:, (per_group + 1) * HD :]

    def scores_of(keys):
        products = lax.dot_general(
            keys, queries, (((1,), (1,)), ((), ())), preferred_element_type=jnp.float32
        )
        return products * scaling

    def weigh(weights, values):
        return lax.dot_general(
            values,
            weights.astype(jnp.bfloat16),
            (((0,), (0,)), ((), ())),
            preferred_element_type=jnp.float32,
        )

    def merge(scores, values):
        old_max = max_ref[...]
        new_max = jnp.maximum(old_max, jnp.max(scores, axis=0, keepdims=True))
        factor = jnp.exp2(old_max - new_max)
        weights = jnp.exp2(scores - new_max)
        max_ref[...] = new_max
        sum_ref[...] = sum_ref[...] * factor + jnp.sum(weights, axis=0, keepdims=True)
        numer_ref[...] = numer_ref[...] * factor + weigh(weights, values)

    key_at = lax.broadcasted_iota(jnp.int32, (new_rows, query_rows), 0)
    token_at = lax.broadcasted_iota(jnp.int32, (new_rows, query_rows), 1) % new_rows
    scores = jnp.where(key_at <= token_at, scores_of(key_new), negative)
    first_max = jnp.max(scores, axis=0, keepdims=True)
    weights = jnp.exp2(scores - first_max)
    max_ref[...] = first_max
    sum_ref[...] = jnp.sum(weights, axis=0, keepdims=True)
    numer_ref[...] = weigh(weights, value_new)

    def visit(step, carried):
        load(step).wait()
        offset = step * block_len

        @pl.when(offset + block_len <= length)
        def _():
            merge(scores_of(rows_ref[step, :, :HD]), rows_ref[step, :, HD:])

        @pl.when(jnp.logical_and(offset < length, offset + block_len > length))
        def _():
            position = offset + lax.broadcasted_iota(jnp.int32, (block_len, query_rows), 0)
            scores = jnp.where(position < length, scores_of(rows_ref[step, :, :HD]), negative)
            merge(scores, rows_ref[step, :, HD:])

        return carried

    lax.fori_loop(0, block_count, visit, 0)

    whole_copy.wait()
    window_rows = window_ref.shape[0]
    tile = window_rows - new_rows
    start = jnp.minimum(length // tile * tile, cache_ref.shape[0] - window_rows)
    start = pl.multiple_of(start, tile)
    fetch = pltpu.make_async_copy(cache_ref.at[pl.ds(start, window_rows)], window_ref, window_sem)
    fetch.start()
    attended = (numer_ref[...] / sum_ref[...]).T.astype(out_ref.dtype)
    for head in range(per_group):
        out_ref[:, head * HD : (head + 1) * HD] = attended[head * new_rows : (head + 1) * new_rows]
    fetch.wait()
    shift = length - start
    fresh = group_ref[:, per_group * HD :].astype(jnp.float32)
    fresh = jnp.concatenate([fresh, jnp.zeros((tile, 2 * HD), jnp.float32)], axis=0)
    fresh = pltpu.roll(fresh, shift, 0)
    row_at = lax.broadcasted_iota(jnp.int32, fresh.shape, 0)
    replaced = jnp.logical_and(row_at >= shift, row_at < shift + new_rows)
    window = jnp.where(replaced, fresh, window_ref[...].astype(jnp.float32))
    window_ref[...] = window.astype(window_ref.dtype)
    store = pltpu.make_async_copy(
        window_ref, appended_ref.at[pl.ds(start, window_rows)], window_sem
    )
    store.start()
    store.wait()


def attend_call(places, lengths, requests, group_cols, cache_rows):
    new_rows = group_cols.shape[0]
    query_rows = HEADS // KVH * new_rows
    cache_len = cache_rows.shape[0]
    block_len = min(512, cache_len)
    vmem = pl.BlockSpec(memory_space=pltpu.VMEM)
    anywhere = pl.BlockSpec(memory_space=pl.ANY)
    return pl.pallas_call(
        attend_kernel,
        out_shape=[
            jax.ShapeDtypeStruct((new_rows, HEADS // KVH * HD), jnp.bfloat16),
            jax.ShapeDtypeStruct(cache_rows.shape, cache_rows.dtype),
        ],
        in_specs=[pl.BlockSpec(memory_space=pltpu.SMEM)] * 3 + [vmem, anywhere],
        out_specs=[vmem, anywhere],
        scratch_shapes=[
            pltpu.VMEM((cache_len // block_len, block_len, 2 * HD), jnp.bfloat16),
            pltpu.VMEM((new_rows + 16, 2 * HD), jnp.bfloat16),
            pltpu.VMEM((HD, query_rows), jnp.float32),
            pltpu.VMEM((1, query_rows), jnp.float32),
            pltpu.VMEM((1, query_rows), jnp.float32),
            pltpu.SemaphoreType.DMA((cache_len // block_len,)),
            pltpu.SemaphoreType.DMA,
            pltpu.SemaphoreType.DMA,
        ],
        compiler_params=pltpu.CompilerParams(vmem_limit_bytes=24 * 1024 * 1024),
        cost_estimate=pl.CostEstimate(
            flops=4 * query_rows * cache_len * HD,
            bytes_accessed=4 * cache_rows.size,
            transcendentals=query_rows * cache_len,
        ),
    )(places, lengths, requests, group_cols, cache_rows)


def project_near_kernel(place_ref, *refs):
    piece_refs, gain_ref, weights = refs[:8], refs[8], refs[9:11]
    normed_ref, out_ref = refs[11:]
    gy_place, z_place, x_place = (place_ref[at] for at in range(3))
    rows, width = piece_refs[0].shape
    squares = jnp.zeros((rows, width), jnp.float32)
    for piece_ref in piece_refs:
        values = piece_ref[...].astype(jnp.float32)
        squares = squares + values * values
    mean_square = jnp.sum(squares, axis=1, keepdims=True) / (len(piece_refs) * width)
    factor = lax.rsqrt(mean_square + epsilon)
    for (far, near), piece_ref in zip(PAIRS, piece_refs):
        block, half = z_place ^ far, x_place ^ near
        values = piece_ref[...].astype(jnp.float32) * factor
        values = values * gain_ref[2 * block + half].astype(jnp.float32)
        normed_ref[block, half] = values.astype(jnp.bfloat16)
    total = jnp.zeros(out_ref.shape, jnp.float32)
    for offset, weight in enumerate(weights):
        for half in range(2):
            total = total + jnp.dot(
                normed_ref[gy_place ^ offset, half],
                weight[half * width : (half + 1) * width],
                preferred_element_type=jnp.float32,
            )
    out_ref[...] = total


def project_far_kernel(place_ref, normed_ref, near_ref, far, far_near, out_ref):
    width = normed_ref.shape[3]
    total = near_ref[...]
    for offset, weight in ((2, far), (3, far_near)):
        for half in range(2):
            total = total + jnp.dot(
                normed_ref[place_ref[0] ^ offset, half],
                weight[half * width : (half + 1) * width],
                preferred_element_type=jnp.float32,
            )
    out_ref[...] = total.astype(out_ref.dtype)


SMEM = pl.BlockSpec(memory_space=pltpu.SMEM)
VMEM = pl.BlockSpec(memory_space=pltpu.VMEM)
ANYWHERE = pl.BlockSpec(memory_space=pl.ANY)


def project_near_call(places, pieces, gain, own, near):
    rows, width = pieces[0].shape
    depth, columns = own.shape
    return pl.pallas_call(
        project_near_kernel,
        out_shape=[
            jax.ShapeDtypeStruct((4, 2, rows, width), jnp.bfloat16),
            jax.ShapeDtypeStruct((rows, columns), jnp.float32),
        ],
        in_specs=[SMEM] + [VMEM] * 11,
        out_specs=[VMEM] * 2,
        compiler_params=pltpu.CompilerParams(vmem_limit_bytes=24 * 1024 * 1024),
        cost_estimate=pl.CostEstimate(
            flops=4 * rows * depth * columns,
            bytes_accessed=4 * depth * columns,
            transcendentals=rows,
        ),
    )(places, *pieces, gain.reshape(len(pieces), 1, width), own, near)


def project_far_call(places, normed, near, far_weights):
    rows, columns = near.shape
    depth = far_weights[0].shape[0]
    return pl.pallas_call(
        project_far_kernel,
        out_shape=jax.ShapeDtypeStruct((rows, columns), jnp.bfloat16),
        in_specs=[SMEM] + [VMEM] * 4,
        out_specs=VMEM,
        compiler_params=pltpu.CompilerParams(vmem_limit_bytes=24 * 1024 * 1024),
        cost_estimate=pl.CostEstimate(
            flops=4 * rows * depth * columns,
            bytes_accessed=4 * depth * columns,
            transcendentals=0,
        ),
    )(places, normed, near, *far_weights)


def out_kernel(place_ref, attended_ref, weight_ref, *out_refs):
    z_place, x_place = place_ref[1], place_ref[2]
    width = out_refs[0].shape[1]
    for (far, near), out_ref in zip(PAIRS, out_refs):
        column = pl.multiple_of((x_place ^ near) * width, width)
        out_ref[...] = jnp.dot(
            attended_ref[z_place ^ far],
            weight_ref[:, pl.ds(column, width)],
            preferred_element_type=jnp.float32,
        ).astype(out_ref.dtype)


def out_call(places, attended, weight):
    slots, rows, depth = attended.shape
    columns = weight.shape[1]
    piece = jax.ShapeDtypeStruct((rows, columns // 2), jnp.bfloat16)
    return pl.pallas_call(
        out_kernel,
        out_shape=[piece] * 8,
        in_specs=[SMEM, VMEM, VMEM],
        out_specs=[VMEM] * 8,
        compiler_params=pltpu.CompilerParams(vmem_limit_bytes=16 * 1024 * 1024),
        cost_estimate=pl.CostEstimate(
            flops=2 * slots * rows * depth * columns,
            bytes_accessed=2 * depth * columns,
            transcendentals=0,
        ),
    )(places, attended, weight)


def up_kernel(place_ref, *refs):
    sources, gain_ref, weight_source = refs[:8], refs[8], refs[9]
    sent_ref, kept_ref, last_ref, scaled_ref, piece_ref, weight_ref, sems = refs[10:]
    copies = [
        pltpu.make_async_copy(source, piece_ref.at[at], sems.at[at])
        for at, source in enumerate(sources)
    ]
    copies.append(pltpu.make_async_copy(weight_source, weight_ref, sems.at[len(sources)]))
    for copy in copies:
        copy.start()
    gy_place, z_place, x_place = (place_ref[at] for at in range(3))
    core = gy_place % 2
    rows, width = piece_ref.shape[1:]
    columns = weight_ref.shape[1]
    ones = jnp.ones((8, width), jnp.float32)
    for far in range(4):
        slot = z_place ^ far
        squares = jnp.zeros((rows, width), jnp.float32)
        for near in range(2):
            half = x_place ^ near
            copies[2 * far + near].wait()
            values = piece_ref[2 * far + near].astype(jnp.float32)
            squares = squares + values * values
            gain = gain_ref[:, pl.ds(pl.multiple_of(half * width, width), width)]
            scaled_ref[slot % 2, half, slot // 2] = (values * gain).astype(jnp.bfloat16)
        sums = lax.dot_general(
            ones,
            squares,
            (((1,), (1,)), ((), ())),
            precision=lax.Precision.HIGHEST,
            preferred_element_type=jnp.float32,
        )
        last_ref[slot, :, columns:] = sums[:1]
    copies[-1].wait()
    step = 512
    for parity, out_ref in ((1 - core, sent_ref), (core, kept_ref)):
        for column in range(0, columns, step):
            total = jnp.zeros((2 * rows, step), jnp.float32)
            for half in range(2):
                total = total + jnp.dot(
                    scaled_ref[parity, half].reshape(2 * rows, width),
                    weight_ref[half * width : (half + 1) * width, column : column + step],
                    preferred_element_type=jnp.float32,
                )
            for pair in range(2):
                last_row = total[(pair + 1) * rows - 1 : (pair + 1) * rows]
                last_ref[2 * pair + parity, :, column : column + step] = last_row
            out_ref[:, :, column : column + step] = total.reshape(2, rows, step).astype(
                out_ref.dtype
            )


def up_call(places, pieces, gain, weight):
    rows, width = pieces[0].shape
    depth, columns = weight.shape
    return pl.pallas_call(
        up_kernel,
        out_shape=[
            jax.ShapeDtypeStruct((2, rows, columns), jnp.bfloat16),
            jax.ShapeDtypeStruct((2, rows, columns), jnp.float32),
            jax.ShapeDtypeStruct((4, 1, columns + rows), jnp.float32),
        ],
        in_specs=[SMEM] + [ANYWHERE] * 8 + [VMEM, ANYWHERE],
        out_specs=[VMEM] * 3,
        scratch_shapes=[
            pltpu.VMEM((2, 2, 2, rows, width), jnp.bfloat16),
            pltpu.VMEM((8, rows, width), jnp.bfloat16),
            pltpu.VMEM((depth, columns), jnp.bfloat16),
            pltpu.SemaphoreType.DMA((9,)),
        ],
        compiler_params=pltpu.CompilerParams(vmem_limit_bytes=48 * 1024 * 1024),
        cost_estimate=pl.CostEstimate(
            flops=8 * rows * depth * columns,
            bytes_accessed=2 * depth * columns,
            transcendentals=0,
        ),
    )(places, *pieces, gain.reshape(1, depth), weight)


def down_kernel(place_ref, active_ref, *refs):
    sources, out_refs, tie_ref, (weight_ref, sems) = refs[:4], refs[4:12], refs[12], refs[13:]
    gy_place, z_place, x_place = (place_ref[at] for at in range(3))
    copies = [
        pltpu.make_async_copy(source, weight_ref.at[at], sems.at[at])
        for at, source in enumerate(sources)
    ]
    for copy in copies:
        copy.start()
    width = out_refs[0].shape[1]
    for copy in copies:
        copy.wait()
    for (far, near), out_ref in zip(PAIRS, out_refs):
        offset = gy_place ^ z_place ^ far
        column = pl.multiple_of((x_place ^ near) * width, width)
        out_ref[...] = jnp.dot(
            active_ref[...],
            weight_ref[offset, :, pl.ds(column, width)],
            preferred_element_type=jnp.float32,
        ).astype(out_ref.dtype)
    tie_ref[...] = jnp.zeros_like(tie_ref)


def down_call(places, active, weights):
    rows, hidden = active.shape
    columns = weights[0].shape[1]
    piece = jax.ShapeDtypeStruct((rows, columns // 2), jnp.bfloat16)
    *pieces, tie = pl.pallas_call(
        down_kernel,
        out_shape=[piece] * 8 + [jax.ShapeDtypeStruct((8, 128), jnp.float32)],
        in_specs=[SMEM, VMEM] + [ANYWHERE] * 4,
        out_specs=[VMEM] * 9,
        scratch_shapes=[
            pltpu.VMEM((4, hidden, columns), jnp.bfloat16),
            pltpu.SemaphoreType.DMA((4,)),
        ],
        compiler_params=pltpu.CompilerParams(vmem_limit_bytes=32 * 1024 * 1024),
        cost_estimate=pl.CostEstimate(
            flops=8 * rows * hidden * columns,
            bytes_accessed=8 * hidden * columns,
            transcendentals=0,
        ),
    )(places, active, *weights)
    return pieces, tie


def head_kernel(rows_ref, weight_ref, out_ref):
    logits = jnp.dot(rows_ref[...], weight_ref[...], preferred_element_type=jnp.float32)

    @pl.when(pl.program_id(0) == 0)
    def _():
        out_ref[...] = logits

    @pl.when(pl.program_id(0) > 0)
    def _():
        out_ref[...] = jnp.maximum(out_ref[...], logits)


def head_call(head_rows, weight, part):
    depth, columns = weight.shape
    step = min(512, columns // 2)
    count = columns // 2 // step
    return pl.pallas_call(
        head_kernel,
        grid=(count,),
        out_shape=jax.ShapeDtypeStruct((head_rows.shape[0], step), jnp.float32),
        in_specs=[
            pl.BlockSpec(head_rows.shape, lambda at: (0, 0)),
            pl.BlockSpec((depth, step), lambda at: (0, part * count + at)),
        ],
        out_specs=pl.BlockSpec((head_rows.shape[0], step), lambda at: (0, 0)),
        compiler_params=pltpu.CompilerParams(vmem_limit_bytes=24 * 1024 * 1024),
        cost_estimate=pl.CostEstimate(
            flops=head_rows.shape[0] * depth * columns,
            bytes_accessed=depth * columns,
            transcendentals=0,
        ),
    )(head_rows, weight)


def stationary(
    tokens,
    attn_gain,
    qkv_weight,
    out_weight,
    mlp_gain,
    up_weight,
    down_weight,
    final_gain,
    head_weight,
    kv_cache,
    cache_lengths,
    slot_request,
):
    gx_count = lax.axis_size("gx")
    gy_count = lax.axis_size("gy")
    device_count = gx_count * gy_count
    gx_place, gy_place = lax.axis_index("gx"), lax.axis_index("gy")
    z_place, x_place, pair_place = gx_place // 2, gx_place % 2, gy_place // 2
    places = jnp.stack([gy_place, z_place, x_place])
    rows, width = tokens.shape
    features = gx_count * width
    own_features, hidden_units = up_weight.shape

    def pick(blocks, place):
        return lax.dynamic_index_in_dim(blocks, place, 0, keepdims=False)

    def to_all(block):
        pieces = jnp.broadcast_to(block[None], (device_count,) + block.shape)
        return exchange(pieces, ("gx", "gy")).reshape((gx_count, gy_count) + block.shape)

    far_qkv = xor_permute(qkv_weight, "gy", 2)
    near_qkv = xor_permute(qkv_weight, "gy", 1)
    normed, near_terms = project_near_call(
        places, gather_blocks(tokens), attn_gain, qkv_weight, near_qkv
    )
    far_qkv, normed, near_terms = lax.optimization_barrier((far_qkv, normed, near_terms))
    far_weights = (far_qkv, xor_permute(far_qkv, "gy", 1))
    group_cols = project_far_call(places, normed, near_terms, far_weights)
    held = transpose_places(tokens)

    attended, appended = attend_call(
        places, cache_lengths, slot_request, group_cols, kv_cache[0]
    )
    new_cache = appended[None]

    attended, held = lax.optimization_barrier((attended, held))
    attention = lax.all_gather(attended, "gy", axis=0)
    sent_weight, attention = lax.optimization_barrier((down_weight, attention))
    far_down = xor_permute(sent_weight, "gy", 2)
    near_down = xor_permute(down_weight, "gy", 1)

    middle = held.astype(jnp.float32) + scatter_blocks(out_call(places, attention, out_weight))
    middle = middle.astype(jnp.bfloat16)

    gain = lax.dynamic_slice_in_dim(mlp_gain, gy_place * own_features, own_features, 0)
    blocks = gather_blocks(middle)
    sent, kept, last_up = up_call(places, blocks, gain.astype(jnp.float32), up_weight)
    moved, _ = lax.optimization_barrier((middle, blocks[-1]))
    middle_slot = transpose_places(moved)
    received = xor_permute(sent, "gy", 1)
    last_up = last_up[:, 0]
    last_up = last_up + xor_permute(last_up, "gy", 1)
    other = pick(kept, 1 - pair_place) + pick(received, 1 - pair_place).astype(jnp.float32)
    other, last_up, middle_slot = lax.optimization_barrier(
        (other.astype(jnp.bfloat16), last_up, middle_slot)
    )
    far_down, _ = lax.optimization_barrier((far_down, other))
    far_near_down = xor_permute(far_down, "gy", 1)
    far_up = xor_permute(other, "gy", 2)
    last_up = last_up + xor_permute(last_up, "gy", 2)
    factors = lax.rsqrt(last_up[:, hidden_units:] / features + epsilon)

    last_active = jnp.maximum(last_up[:, :hidden_units] * factors[:, rows - 1 :], 0.0)
    last_terms = rows_dot((last_active * last_active).astype(jnp.bfloat16), down_weight)
    last_row = middle[rows - 1 :].astype(jnp.float32)
    blank = jnp.zeros_like(last_terms)
    last_terms = last_terms + lax.dynamic_update_slice(
        blank, last_row, (z_place, x_place * width)
    )
    last_pieces = to_all(last_terms.astype(jnp.bfloat16))

    up_values = pick(kept, pair_place) + pick(received, pair_place).astype(jnp.float32)
    up_values = up_values + far_up.astype(jnp.float32)
    rectified = jnp.maximum(up_values * pick(factors, gy_place)[:, None], 0.0)
    activation = (rectified * rectified).astype(jnp.bfloat16)
    down_weights = (down_weight, near_down, far_down, far_near_down)
    pieces, tie = down_call(places, activation, down_weights)
    last_pieces, _ = lax.optimization_barrier((last_pieces, tie))
    last_hidden = jnp.sum(last_pieces.astype(jnp.float32), axis=0)
    last_hidden = last_hidden.transpose(1, 0, 2).reshape(gy_count, features)
    last_hidden = last_hidden.astype(jnp.bfloat16).astype(jnp.float32)
    mean_square = jnp.mean(last_hidden * last_hidden, axis=1)
    last_norms = jnp.sqrt(mean_square)
    head_input = (
        last_hidden * lax.rsqrt(mean_square + epsilon)[:, None] * final_gain.astype(jnp.float32)
    ).astype(jnp.bfloat16)
    first_max = head_call(head_input, head_weight, 0)
    second_max = head_call(head_input, head_weight, 1)
    largest = jnp.max(jnp.maximum(first_max, second_max), axis=1)
    max_logits = jnp.max(to_all(largest), axis=(0, 1))

    hidden_terms = scatter_blocks(pieces, first_max)
    hidden_out = (middle_slot.astype(jnp.float32) + hidden_terms).astype(jnp.bfloat16)
    return (hidden_out, new_cache, last_norms, max_logits, head_input)


def solution(mesh):
    gx_count, gy_count = mesh.shape["gx"], mesh.shape["gy"]
    body = stationary if gx_count == KVH and gy_count == 4 else local
    in_specs = (
        P("gy", "gx"),
        P(),
        P("gy", "gx"),
        P("gx", "gy"),
        P(),
        P("gy", "gx"),
        P("gx", "gy"),
        P(),
        P(None, ("gx", "gy")),
        P(("gy", "gx"), None, None),
        P(),
        P(),
    )
    out_specs = (P("gy", "gx"), P(("gy", "gx"), None, None), P(), P(), P())
    return jax.shard_map(body, mesh=mesh, in_specs=in_specs, out_specs=out_specs, check_vma=False)
```

```python
import functools
import math

import jax
import jax.numpy as jnp
from jax import lax
from jax.experimental import pallas as pl
from jax.experimental.pallas import tpu as pltpu
from jax.sharding import PartitionSpec as P

HEADS = 32
KVH = 8
HD = 128


epsilon = 1e-05
negative = -1e30


def from_partner(block, axis, distance):
    count = lax.axis_size(axis)
    route = []
    for low in range(count):
        high = low | 1 << distance
        if high != low and high < count:
            route += [(low, high), (high, low)]
    return lax.ppermute(block, axis, route)


def rms_factor(row_block):
    return lax.rsqrt(jnp.mean(row_block * row_block, axis=-1, keepdims=True) + epsilon)


def gather_features(shard_rows):
    return lax.all_gather(shard_rows, "gx", axis=1, tiled=True)


def rows_product(left_rows, weight_shard):
    return jnp.dot(
        left_rows,
        lax.all_gather(weight_shard, "gy", axis=0, tiled=True),
        preferred_element_type=jnp.float32,
    )


def columns_product(left_rows, weight_shard):
    return jnp.dot(
        left_rows,
        lax.all_gather(weight_shard, "gy", axis=1, tiled=True),
        preferred_element_type=jnp.float32,
    )


def pair_swap(values):
    return from_partner(values, "gx", KVH.bit_length() - 1)


def scatter_partials(partial_terms):
    return lax.psum_scatter(
        partial_terms.astype(jnp.bfloat16), "gx", scatter_dimension=1, tiled=True
    ).astype(jnp.float32)


def merge_block(carried, scores, value_rows):
    row_max, running, numerator = carried
    new_max = jnp.maximum(row_max, jnp.max(scores, axis=1, keepdims=True))
    factor = jnp.exp(row_max - new_max)
    weights = jnp.exp(scores - new_max)
    running = running * factor + jnp.sum(weights, axis=1, keepdims=True)
    numerator = numerator * factor + jnp.dot(
        weights.astype(jnp.bfloat16), value_rows, preferred_element_type=jnp.float32
    )
    return (new_max, running, numerator)


def attend_cache(group_cols, cache_rows, length, new_rows):
    per_group = HEADS // KVH
    scaling = 1.0 / math.sqrt(HD)
    query_rows = per_group * new_rows
    queries = (
        group_cols[:, : per_group * HD]
        .reshape(new_rows, per_group, HD)
        .transpose(1, 0, 2)
        .reshape(query_rows, HD)
    )
    key_new = group_cols[:, per_group * HD : (per_group + 1) * HD]
    value_new = group_cols[:, (per_group + 1) * HD :]
    block_len = min(512, cache_rows.shape[0])

    def visit_block(step_index, carried):
        offset = step_index * block_len
        block_rows = lax.dynamic_slice_in_dim(cache_rows, offset, block_len, 0)
        scores = (
            jnp.dot(queries, block_rows[:, :HD].T, preferred_element_type=jnp.float32) * scaling
        )
        positions = offset + jnp.arange(block_len)
        scores = jnp.where(positions[None, :] < length, scores, negative)
        return merge_block(carried, scores, block_rows[:, HD:])

    initial = (
        jnp.full((query_rows, 1), negative, jnp.float32),
        jnp.zeros((query_rows, 1), jnp.float32),
        jnp.zeros((query_rows, HD), jnp.float32),
    )
    block_count = (length + block_len - 1) // block_len
    carried = lax.fori_loop(0, block_count, visit_block, initial)
    new_scores = jnp.dot(queries, key_new.T, preferred_element_type=jnp.float32) * scaling
    causal = jnp.arange(new_rows)[None, :] <= (jnp.arange(query_rows) % new_rows)[:, None]
    new_scores = jnp.where(causal, new_scores, negative)
    row_max, running, numerator = merge_block(carried, new_scores, value_new)
    attended = (numerator / running).astype(jnp.bfloat16)
    attended = (
        attended.reshape(per_group, new_rows, HD)
        .transpose(1, 0, 2)
        .reshape(new_rows, per_group * HD)
    )
    fresh = jnp.concatenate([key_new, value_new], axis=1)
    appended = lax.dynamic_update_slice(cache_rows, fresh, (length, jnp.zeros((), jnp.int32)))
    return (attended, appended)


def local(
    tokens,
    attn_gain,
    qkv_weight,
    out_weight,
    mlp_gain,
    up_weight,
    down_weight,
    final_gain,
    head_weight,
    kv_cache,
    cache_lengths,
    slot_request,
):
    gx_count = lax.axis_size("gx")
    gy_count = lax.axis_size("gy")
    copies = gx_count // KVH
    gx_place = lax.axis_index("gx")
    copy_index = gx_place // KVH
    slot_index = lax.axis_index("gy") * copies + copy_index
    new_rows = tokens.shape[0] // copies
    feature_cols = tokens.shape[1]
    gathered_tokens = gather_features(tokens)
    tokens_f32 = gathered_tokens.astype(jnp.float32)
    normed = (tokens_f32 * rms_factor(tokens_f32) * attn_gain.astype(jnp.float32)).astype(
        jnp.bfloat16
    )
    projected = rows_product(normed, qkv_weight).astype(jnp.bfloat16)
    if copies == 2:
        own_half = lax.dynamic_slice_in_dim(projected, copy_index * new_rows, new_rows, 0)
        sent_rows = lax.dynamic_slice_in_dim(projected, (1 - copy_index) * new_rows, new_rows, 0)
        received = pair_swap(sent_rows)
        group_cols = jnp.where(
            copy_index == 0,
            jnp.concatenate([own_half, received], axis=1),
            jnp.concatenate([received, own_half], axis=1),
        )
    else:
        group_cols = projected
    length = cache_lengths[slot_request[slot_index]]
    attended, appended = attend_cache(group_cols, kv_cache[0], length, new_rows)
    new_cache = appended[None]
    if copies == 2:
        half_width = attended.shape[1] // 2
        kept_half = lax.dynamic_slice_in_dim(attended, copy_index * half_width, half_width, 1)
        handed = lax.dynamic_slice_in_dim(attended, (1 - copy_index) * half_width, half_width, 1)
        returned = pair_swap(handed)
        attention_rows = jnp.where(
            copy_index == 0,
            jnp.concatenate([kept_half, returned], axis=0),
            jnp.concatenate([returned, kept_half], axis=0),
        )
    else:
        attention_rows = attended
    attention_terms = columns_product(attention_rows, out_weight)
    middle = (tokens.astype(jnp.float32) + scatter_partials(attention_terms)).astype(jnp.bfloat16)
    middle_full = gather_features(middle)
    middle_f32 = middle_full.astype(jnp.float32)
    mlp_input = (middle_f32 * rms_factor(middle_f32) * mlp_gain.astype(jnp.float32)).astype(
        jnp.bfloat16
    )
    up_values = rows_product(mlp_input, up_weight)
    rectified = jnp.maximum(up_values, 0.0)
    activation = (rectified * rectified).astype(jnp.bfloat16)
    down_terms = columns_product(activation, down_weight)
    hidden_out = (middle.astype(jnp.float32) + scatter_partials(down_terms)).astype(jnp.bfloat16)
    final_rows = hidden_out.reshape(copies, new_rows, feature_cols)[:, new_rows - 1, :]
    every_last = lax.all_gather(final_rows, ("gx", "gy"), axis=0, tiled=True)
    slot_rows = every_last.reshape(gx_count, gy_count, copies, feature_cols).transpose(1, 2, 0, 3)
    slot_rows = slot_rows.reshape(gy_count * copies, gx_count * feature_cols).astype(jnp.float32)
    mean_square = jnp.mean(slot_rows * slot_rows, axis=1)
    last_norms = jnp.sqrt(mean_square)
    head_input = (
        slot_rows * lax.rsqrt(mean_square + epsilon)[:, None] * final_gain.astype(jnp.float32)
    ).astype(jnp.bfloat16)
    logits = jnp.dot(head_input, head_weight, preferred_element_type=jnp.float32)
    max_logits = lax.pmax(jnp.max(logits, axis=1), ("gx", "gy"))
    return (hidden_out, new_cache, last_norms, max_logits, head_input)


def xor_permute(values, axis, distance):
    count = lax.axis_size(axis)
    return lax.ppermute(values, axis, [(place, place ^ distance) for place in range(count)])


def transpose_places(block):
    gx_count, gy_count = lax.axis_size("gx"), lax.axis_size("gy")
    route = []
    for gx_at in range(gx_count):
        for gy_at in range(gy_count):
            gx_to = gy_at // 2 * 4 + gx_at % 4
            gy_to = gx_at // 4 * 2 + gy_at % 2
            route.append((gx_at * gy_count + gy_at, gx_to * gy_count + gy_to))
    return lax.ppermute(block, ("gx", "gy"), route)


def exchange(blocks, axes):
    return lax.all_to_all(blocks, axes, split_axis=0, concat_axis=0, tiled=True)


def across(block, places):
    return xor_permute(block, "gx", places)


PAIRS = tuple((far, near) for far in range(4) for near in range(2))
SENT_ORDER = (5, 7, 4, 6, 3, 2, 1, 0)


def gather_blocks(block):
    found = {(0, 0): block, (0, 1): across(block, 1)}
    for far in (1, 2, 3):
        found[far, 0] = across(block, 2 * far)
    for far in (1, 2, 3):
        found[far, 1] = across(found[far, 0], 1)
    return [found[at] for at in PAIRS]


def scatter_blocks(blocks, tie=None):
    held = dict(zip(PAIRS, blocks))

    def wide(values):
        return values.astype(jnp.float32)

    pairs = [wide(held[far, 0]) + wide(across(held[far, 1], 1)) for far in (2, 3)]
    pairs = [pair.astype(jnp.bfloat16) for pair in pairs]
    if tie is not None:
        *pairs, tie = lax.optimization_barrier((*pairs, tie))
    pairs[0], diagonal, beside = lax.optimization_barrier((pairs[0], held[1, 1], held[0, 1]))
    summed = [across(pair, 2 * far) for far, pair in zip((2, 3), pairs)]
    near = wide(across(held[1, 0], 2)) + wide(across(diagonal, 3))
    near = near + wide(held[0, 0]) + wide(across(beside, 1))
    return near + wide(summed[0]) + wide(summed[1]), tie


def rows_dot(left, weight):
    return lax.dot_general(
        left, weight, (((left.ndim - 1,), (0,)), ((), ())), preferred_element_type=jnp.float32
    )


def row_factors(squares, features):
    factors = lax.rsqrt(squares / features + epsilon)
    rows = factors.shape[1]
    return jnp.broadcast_to(factors, (rows, rows)).T[:, :1]


def attend_kernel(
    features,
    place_ref,
    lengths_ref,
    requests_ref,
    kept_ref,
    received_ref,
    squares_ref,
    cache_ref,
    out_ref,
    appended_ref,
    group_ref,
    rows_ref,
    window_ref,
    numer_ref,
    max_ref,
    sum_ref,
    load_sems,
    copy_sem,
    window_sem,
):
    per_group = HEADS // KVH
    new_rows = group_ref.shape[0]
    query_rows = per_group * new_rows
    block_len = rows_ref.shape[1]
    block_count = rows_ref.shape[0]
    scaling = math.log2(math.e) / math.sqrt(HD)
    length = lengths_ref[requests_ref[place_ref[0]]]

    def load(step):
        source = cache_ref.at[pl.ds(pl.multiple_of(step * block_len, block_len), block_len)]
        return pltpu.make_async_copy(source, rows_ref.at[step], load_sems.at[step])

    for step in range(block_count):
        load(step).start()
    whole_copy = pltpu.make_async_copy(cache_ref, appended_ref, copy_sem)
    whole_copy.start()
    projected = kept_ref[...] + received_ref[...].astype(jnp.float32)
    projected = projected * row_factors(squares_ref[...], features)
    group_ref[...] = projected.astype(group_ref.dtype)
    queries = jnp.concatenate(
        [group_ref[:, head * HD : (head + 1) * HD] for head in range(per_group)], axis=0
    )
    key_new = group_ref[:, per_group * HD : (per_group + 1) * HD]
    value_new = group_ref[:, (per_group + 1) * HD :]

    def scores_of(keys):
        products = lax.dot_general(
            keys, queries, (((1,), (1,)), ((), ())), preferred_element_type=jnp.float32
        )
        return products * scaling

    def weigh(weights, values):
        return lax.dot_general(
            values,
            weights.astype(jnp.bfloat16),
            (((0,), (0,)), ((), ())),
            preferred_element_type=jnp.float32,
        )

    def merge(scores, values):
        old_max = max_ref[...]
        new_max = jnp.maximum(old_max, jnp.max(scores, axis=0, keepdims=True))
        factor = jnp.exp2(old_max - new_max)
        weights = jnp.exp2(scores - new_max)
        max_ref[...] = new_max
        sum_ref[...] = sum_ref[...] * factor + jnp.sum(weights, axis=0, keepdims=True)
        numer_ref[...] = numer_ref[...] * factor + weigh(weights, values)

    key_at = lax.broadcasted_iota(jnp.int32, (new_rows, query_rows), 0)
    token_at = lax.broadcasted_iota(jnp.int32, (new_rows, query_rows), 1) % new_rows
    scores = jnp.where(key_at <= token_at, scores_of(key_new), negative)
    first_max = jnp.max(scores, axis=0, keepdims=True)
    weights = jnp.exp2(scores - first_max)
    max_ref[...] = first_max
    sum_ref[...] = jnp.sum(weights, axis=0, keepdims=True)
    numer_ref[...] = weigh(weights, value_new)

    def visit(step, carried):
        load(step).wait()
        offset = step * block_len

        @pl.when(offset + block_len <= length)
        def _():
            merge(scores_of(rows_ref[step, :, :HD]), rows_ref[step, :, HD:])

        @pl.when(jnp.logical_and(offset < length, offset + block_len > length))
        def _():
            position = offset + lax.broadcasted_iota(jnp.int32, (block_len, query_rows), 0)
            scores = jnp.where(position < length, scores_of(rows_ref[step, :, :HD]), negative)
            merge(scores, rows_ref[step, :, HD:])

        return carried

    lax.fori_loop(0, block_count, visit, 0)

    whole_copy.wait()
    window_rows = window_ref.shape[0]
    tile = window_rows - new_rows
    start = jnp.minimum(length // tile * tile, cache_ref.shape[0] - window_rows)
    start = pl.multiple_of(start, tile)
    fetch = pltpu.make_async_copy(cache_ref.at[pl.ds(start, window_rows)], window_ref, window_sem)
    fetch.start()
    attended = (numer_ref[...] / sum_ref[...]).T.astype(out_ref.dtype)
    for head in range(per_group):
        out_ref[:, head * HD : (head + 1) * HD] = attended[head * new_rows : (head + 1) * new_rows]
    fetch.wait()
    shift = length - start
    fresh = group_ref[:, per_group * HD :].astype(jnp.float32)
    fresh = jnp.concatenate([fresh, jnp.zeros((tile, 2 * HD), jnp.float32)], axis=0)
    fresh = pltpu.roll(fresh, shift, 0)
    row_at = lax.broadcasted_iota(jnp.int32, fresh.shape, 0)
    replaced = jnp.logical_and(row_at >= shift, row_at < shift + new_rows)
    window = jnp.where(replaced, fresh, window_ref[...].astype(jnp.float32))
    window_ref[...] = window.astype(window_ref.dtype)
    store = pltpu.make_async_copy(
        window_ref, appended_ref.at[pl.ds(start, window_rows)], window_sem
    )
    store.start()
    store.wait()


def attend_call(places, lengths, requests, kept, received, squares, cache_rows, features):
    new_rows = kept.shape[0]
    query_rows = HEADS // KVH * new_rows
    cache_len = cache_rows.shape[0]
    block_len = min(512, cache_len)
    vmem = pl.BlockSpec(memory_space=pltpu.VMEM)
    anywhere = pl.BlockSpec(memory_space=pl.ANY)
    return pl.pallas_call(
        functools.partial(attend_kernel, features),
        out_shape=[
            jax.ShapeDtypeStruct((new_rows, HEADS // KVH * HD), jnp.bfloat16),
            jax.ShapeDtypeStruct(cache_rows.shape, cache_rows.dtype),
        ],
        in_specs=[pl.BlockSpec(memory_space=pltpu.SMEM)] * 3 + [vmem] * 3 + [anywhere],
        out_specs=[vmem, anywhere],
        scratch_shapes=[
            pltpu.VMEM(kept.shape, jnp.bfloat16),
            pltpu.VMEM((cache_len // block_len, block_len, 2 * HD), jnp.bfloat16),
            pltpu.VMEM((new_rows + 16, 2 * HD), jnp.bfloat16),
            pltpu.VMEM((HD, query_rows), jnp.float32),
            pltpu.VMEM((1, query_rows), jnp.float32),
            pltpu.VMEM((1, query_rows), jnp.float32),
            pltpu.SemaphoreType.DMA((cache_len // block_len,)),
            pltpu.SemaphoreType.DMA,
            pltpu.SemaphoreType.DMA,
        ],
        compiler_params=pltpu.CompilerParams(vmem_limit_bytes=12 * 1024 * 1024),
        cost_estimate=pl.CostEstimate(
            flops=4 * query_rows * cache_len * HD,
            bytes_accessed=4 * cache_rows.size,
            transcendentals=query_rows * cache_len,
        ),
    )(places, lengths, requests, kept, received, squares, cache_rows)


SMEM = pl.BlockSpec(memory_space=pltpu.SMEM)
VMEM = pl.BlockSpec(memory_space=pltpu.VMEM)
HBM = pl.BlockSpec(memory_space=pltpu.HBM)


def in_hbm(values):
    return [pltpu.with_memory_space_constraint(value, pltpu.HBM) for value in values]


def start_copies(sources, targets, sems):
    copies = [
        pltpu.make_async_copy(source, target, sems.at[at])
        for at, (source, target) in enumerate(zip(sources, targets))
    ]
    for copy in copies:
        copy.start()
    return copies


def rows_kernel(place_ref, *refs):
    sources, gain_ref, weights = refs[:8], refs[8], refs[9:11]
    sent_out, kept_out, last_ref = refs[11:14]
    sent_ref, kept_ref, scaled_ref, piece_ref, weight_ref, sems, out_sems = refs[14:]
    copies = start_copies(
        [*sources, *weights],
        [piece_ref.at[at] for at in range(8)] + [weight_ref.at[at] for at in range(2)],
        sems,
    )
    gy_place, z_place, x_place = (place_ref[at] for at in range(3))
    core, pair = gy_place % 2, gy_place // 2
    rows, width = piece_ref.shape[1:]
    columns = weight_ref.shape[2]
    ones = jnp.ones((8, width), jnp.float32)
    squares = [jnp.zeros((rows, width), jnp.float32) for _ in range(2)]
    for far in (0, 1, 2, 3):
        block = (z_place ^ far) % 2
        slot = ((z_place ^ far) // 2) ^ pair
        for near in range(2):
            half = x_place ^ near
            copies[2 * far + near].wait()
            values = piece_ref[2 * far + near].astype(jnp.float32)
            squares[far // 2] = squares[far // 2] + values * values
            column = pl.multiple_of((2 * block + half) * width, width)
            gain = gain_ref[:, pl.ds(column, width)]
            scaled_ref[block ^ core, half, slot] = (values * gain).astype(jnp.bfloat16)
    for high in range(2):
        sums = lax.dot_general(
            ones,
            squares[high],
            (((1,), (1,)), ((), ())),
            precision=lax.Precision.HIGHEST,
            preferred_element_type=jnp.float32,
        )
        last_ref[(z_place // 2) ^ high ^ pair, :, columns:] = sums[:1]
    copies[8].wait()
    copies[9].wait()
    step = 256
    for column in range(0, columns, step):
        total = jnp.zeros((2 * rows, step), jnp.float32)
        for block in range(2):
            for half in range(2):
                total = total + jnp.dot(
                    scaled_ref[block, half].reshape(2 * rows, width),
                    weight_ref[block, half * width : (half + 1) * width, column : column + step],
                    preferred_element_type=jnp.float32,
                )
        kept_ref[:, column : column + step] = total[:rows]
        sent_ref[:, column : column + step] = total[rows:].astype(sent_ref.dtype)
        last_ref[0, :, column : column + step] = total[rows - 1 : rows]
        last_ref[1, :, column : column + step] = total[2 * rows - 1 :]
    for copy in start_copies([sent_ref, kept_ref], [sent_out, kept_out], out_sems):
        copy.wait()


def rows_call(places, pieces, gain, own, near):
    rows, width = pieces[0].shape
    depth, columns = own.shape
    return pl.pallas_call(
        rows_kernel,
        out_shape=[
            pltpu.HBM((rows, columns), jnp.bfloat16),
            pltpu.HBM((rows, columns), jnp.float32),
            jax.ShapeDtypeStruct((2, 1, columns + rows), jnp.float32),
        ],
        in_specs=[SMEM] + [HBM] * 8 + [VMEM] + [HBM] * 2,
        out_specs=[HBM] * 2 + [VMEM],
        scratch_shapes=[
            pltpu.VMEM((rows, columns), jnp.bfloat16),
            pltpu.VMEM((rows, columns), jnp.float32),
            pltpu.VMEM((2, 2, 2, rows, width), jnp.bfloat16),
            pltpu.VMEM((8, rows, width), jnp.bfloat16),
            pltpu.VMEM((2, depth, columns), jnp.bfloat16),
            pltpu.SemaphoreType.DMA((10,)),
            pltpu.SemaphoreType.DMA((2,)),
        ],
        compiler_params=pltpu.CompilerParams(vmem_limit_bytes=48 * 1024 * 1024),
        cost_estimate=pl.CostEstimate(
            flops=8 * rows * depth * columns,
            bytes_accessed=4 * depth * columns,
            transcendentals=0,
        ),
    )(places, *in_hbm(pieces), gain.reshape(1, 2 * depth), *in_hbm((own, near)))


def out_kernel(place_ref, attended_ref, other_ref, own, near, *refs):
    out_refs, (slots_ref, weight_ref, piece_ref, sems, out_sems) = refs[:8], refs[8:]
    copies = start_copies(
        [attended_ref, other_ref, own, near],
        [slots_ref.at[0], slots_ref.at[1], weight_ref.at[0], weight_ref.at[1]],
        sems,
    )
    gy_place, z_place, x_place = (place_ref[at] for at in range(3))
    core, pair = gy_place % 2, gy_place // 2
    width = out_refs[0].shape[1]
    for copy in copies:
        copy.wait()
    copies = []
    for at in SENT_ORDER:
        far, near_bit = PAIRS[at]
        block = ((z_place ^ far) % 2) ^ core
        slot = ((z_place ^ far) // 2) ^ pair
        column = pl.multiple_of((x_place ^ near_bit) * width, width)
        piece_ref[at] = jnp.dot(
            slots_ref[slot],
            weight_ref[block, :, pl.ds(column, width)],
            preferred_element_type=jnp.float32,
        ).astype(piece_ref.dtype)
        copies.append(pltpu.make_async_copy(piece_ref.at[at], out_refs[at], out_sems.at[at]))
        copies[-1].start()
    for copy in copies:
        copy.wait()


def out_call(places, attended, other, own, near):
    rows, depth = attended.shape
    columns = own.shape[1]
    piece = pltpu.HBM((rows, columns // 2), jnp.bfloat16)
    return pl.pallas_call(
        out_kernel,
        out_shape=[piece] * 8,
        in_specs=[SMEM] + [HBM] * 4,
        out_specs=[HBM] * 8,
        scratch_shapes=[
            pltpu.VMEM((2, rows, depth), jnp.bfloat16),
            pltpu.VMEM((2, depth, columns), jnp.bfloat16),
            pltpu.VMEM((8, rows, columns // 2), jnp.bfloat16),
            pltpu.SemaphoreType.DMA((4,)),
            pltpu.SemaphoreType.DMA((8,)),
        ],
        compiler_params=pltpu.CompilerParams(vmem_limit_bytes=48 * 1024 * 1024),
        cost_estimate=pl.CostEstimate(
            flops=8 * rows * depth * columns,
            bytes_accessed=4 * depth * columns,
            transcendentals=0,
        ),
    )(places, *in_hbm((attended, other, own, near)))


def down_kernel(features, place_ref, squares_ref, *refs):
    sources, out_refs, tie_ref = refs[:8], refs[8:16], refs[16]
    kept_ref, received_ref, active_ref, weight_ref, piece_ref, sems, out_sems = refs[17:]
    split = sources[4].shape[0]
    rows, hidden = kept_ref.shape
    head, tail = pl.ds(0, split), pl.ds(split, hidden - split)
    copies = start_copies(
        sources,
        [
            kept_ref,
            received_ref,
            weight_ref.at[0],
            weight_ref.at[1],
            weight_ref.at[2, head],
            weight_ref.at[3, head],
            weight_ref.at[2, tail],
            weight_ref.at[3, tail],
        ],
        sems,
    )
    gy_place, z_place, x_place = (place_ref[at] for at in range(3))
    copies[0].wait()
    copies[1].wait()
    up_values = kept_ref[...] + received_ref[...].astype(jnp.float32)
    rectified = jnp.maximum(up_values * row_factors(squares_ref[...], features), 0.0)
    active_ref[...] = (rectified * rectified).astype(active_ref.dtype)
    for copy in copies[2:]:
        copy.wait()
    width = piece_ref.shape[2]
    copies = []
    for at in SENT_ORDER:
        far, near_bit = PAIRS[at]
        offset = gy_place ^ z_place ^ far
        column = pl.multiple_of((x_place ^ near_bit) * width, width)
        piece_ref[at] = jnp.dot(
            active_ref[...],
            weight_ref[offset, :, pl.ds(column, width)],
            preferred_element_type=jnp.float32,
        ).astype(piece_ref.dtype)
        copies.append(pltpu.make_async_copy(piece_ref.at[at], out_refs[at], out_sems.at[at]))
        copies[-1].start()
    tie_ref[...] = jnp.zeros_like(tie_ref)
    for copy in copies:
        copy.wait()


def down_call(places, kept, received, squares, weights, features):
    rows, hidden = kept.shape
    columns = weights[0].shape[1]
    piece = pltpu.HBM((rows, columns // 2), jnp.bfloat16)
    *pieces, tie = pl.pallas_call(
        functools.partial(down_kernel, features),
        out_shape=[piece] * 8 + [jax.ShapeDtypeStruct((8, 128), jnp.float32)],
        in_specs=[SMEM, VMEM] + [HBM] * 8,
        out_specs=[HBM] * 8 + [VMEM],
        scratch_shapes=[
            pltpu.VMEM((rows, hidden), jnp.float32),
            pltpu.VMEM((rows, hidden), jnp.bfloat16),
            pltpu.VMEM((rows, hidden), jnp.bfloat16),
            pltpu.VMEM((4, hidden, columns), jnp.bfloat16),
            pltpu.VMEM((8, rows, columns // 2), jnp.bfloat16),
            pltpu.SemaphoreType.DMA((8,)),
            pltpu.SemaphoreType.DMA((8,)),
        ],
        compiler_params=pltpu.CompilerParams(vmem_limit_bytes=48 * 1024 * 1024),
        cost_estimate=pl.CostEstimate(
            flops=8 * rows * hidden * columns,
            bytes_accessed=8 * hidden * columns,
            transcendentals=0,
        ),
    )(places, squares, *in_hbm((kept, received, *weights)))
    return pieces, tie


def head_kernel(rows_ref, weight_ref, out_ref):
    logits = jnp.dot(rows_ref[...], weight_ref[...], preferred_element_type=jnp.float32)

    @pl.when(pl.program_id(0) == 0)
    def _():
        out_ref[...] = logits

    @pl.when(pl.program_id(0) > 0)
    def _():
        out_ref[...] = jnp.maximum(out_ref[...], logits)


def head_call(head_rows, weight, part, parts):
    depth, columns = weight.shape
    step = min(1024, columns // parts)
    count = columns // parts // step
    return pl.pallas_call(
        head_kernel,
        grid=(count,),
        out_shape=jax.ShapeDtypeStruct((head_rows.shape[0], step), jnp.float32),
        in_specs=[
            pl.BlockSpec(head_rows.shape, lambda at: (0, 0)),
            pl.BlockSpec((depth, step), lambda at: (0, part * count + at)),
        ],
        out_specs=pl.BlockSpec((head_rows.shape[0], step), lambda at: (0, 0)),
        compiler_params=pltpu.CompilerParams(vmem_limit_bytes=48 * 1024 * 1024),
        cost_estimate=pl.CostEstimate(
            flops=2 * head_rows.shape[0] * depth * columns // parts,
            bytes_accessed=2 * depth * columns // parts,
            transcendentals=0,
        ),
    )(head_rows, weight)


def stationary(
    tokens,
    attn_gain,
    qkv_weight,
    out_weight,
    mlp_gain,
    up_weight,
    down_weight,
    final_gain,
    head_weight,
    kv_cache,
    cache_lengths,
    slot_request,
):
    gx_count = lax.axis_size("gx")
    gy_count = lax.axis_size("gy")
    device_count = gx_count * gy_count
    gx_place, gy_place = lax.axis_index("gx"), lax.axis_index("gy")
    z_place, x_place = gx_place // 2, gx_place % 2
    pair_place, core_place = gy_place // 2, gy_place % 2
    places = jnp.stack([gy_place, z_place, x_place])
    rows, width = tokens.shape
    features = gx_count * width
    own_features, hidden_units = up_weight.shape

    def to_all(block):
        pieces = jnp.broadcast_to(block[None], (device_count,) + block.shape)
        return exchange(pieces, ("gx", "gy")).reshape((gx_count, gy_count) + block.shape)

    def chip_gain(gain):
        start = pair_place * 2 * own_features
        return lax.dynamic_slice_in_dim(gain, start, 2 * own_features, 0).astype(jnp.float32)

    def absolute(values, place):
        swapped = jnp.stack([values[1], values[0]])
        return jnp.where(place == 0, values, swapped)

    early = hidden_units // 3
    held, near_qkv, early_rows, late_rows = lax.optimization_barrier(
        (
            transpose_places(tokens),
            xor_permute(qkv_weight, "gy", 1),
            down_weight[:early],
            down_weight[early:],
        )
    )
    early_far = xor_permute(early_rows, "gy", 2)
    blocks = gather_blocks(held)
    sent, kept, last = rows_call(
        places, blocks, chip_gain(attn_gain), qkv_weight, near_qkv
    )
    sent, early_far, out_source, up_source, down_source = lax.optimization_barrier(
        (sent, early_far, out_weight, up_weight, down_weight)
    )
    near_out, near_up, near_down, early_near = (
        xor_permute(part, "gy", 1) for part in (out_source, up_source, down_source, early_far)
    )
    received = xor_permute(sent, "gy", 2)
    squares = last[:, :, qkv_weight.shape[1] :]
    squares = squares[0] + xor_permute(squares[1], "gy", 2)
    attended, appended = attend_call(
        places, cache_lengths, slot_request, kept, received, squares, kv_cache[0], features
    )
    new_cache = appended[None]

    other = xor_permute(attended, "gy", 2)
    late_rows, other, near_out, near_up, near_down, early_near = lax.optimization_barrier(
        (late_rows, other, near_out, near_up, near_down, early_near)
    )
    late_far = xor_permute(late_rows, "gy", 2)
    terms, _ = scatter_blocks(out_call(places, attended, other, out_weight, near_out))
    middle = (held.astype(jnp.float32) + terms).astype(jnp.bfloat16)
    sent, kept, last = rows_call(
        places, gather_blocks(middle), chip_gain(mlp_gain), up_weight, near_up
    )
    received = xor_permute(sent, "gy", 2)
    last = last[:, 0]
    last = last + xor_permute(last[::-1], "gy", 2)
    squares = last[:, hidden_units:]
    late_near = xor_permute(late_far, "gy", 1)
    middle_slot = transpose_places(middle)

    factors = lax.rsqrt(squares[:, rows - 1 :] / features + epsilon)
    last_active = jnp.maximum(last[:, :hidden_units] * factors, 0.0)
    last_active = (last_active * last_active).astype(jnp.bfloat16)
    last_terms = jnp.stack([rows_dot(last_active, part) for part in (down_weight, near_down)])
    last_terms = absolute(absolute(last_terms, core_place).transpose(1, 0, 2), pair_place)
    last_row = middle[rows - 1 :].astype(jnp.float32)[None]
    place = (z_place // 2, z_place % 2, x_place * width)
    last_terms += lax.dynamic_update_slice(jnp.zeros_like(last_terms), last_row, place)
    last_pieces = to_all(last_terms.astype(jnp.bfloat16))

    weights = (down_weight, near_down, early_far, early_near, late_far, late_near)
    pieces, tie = down_call(places, kept, received, squares[:1], weights, features)
    last_pieces, tie, middle_slot = lax.optimization_barrier((last_pieces, tie, middle_slot))
    last_hidden = jnp.sum(last_pieces.astype(jnp.float32), axis=0)
    last_hidden = last_hidden.reshape(2, 2, 2, 2, own_features).transpose(2, 1, 0, 3, 4)
    last_hidden = last_hidden.reshape(gy_count, features)
    last_hidden = last_hidden.astype(jnp.bfloat16).astype(jnp.float32)
    mean_square = jnp.mean(last_hidden * last_hidden, axis=1)
    last_norms = jnp.sqrt(mean_square)
    head_input = (
        last_hidden * lax.rsqrt(mean_square + epsilon)[:, None] * final_gain.astype(jnp.float32)
    ).astype(jnp.bfloat16)
    first_max = head_call(head_input, head_weight, 0, 2)
    hidden_terms, first_max = scatter_blocks(pieces, first_max)
    second_max = head_call(head_input, head_weight, 1, 2)
    largest = jnp.max(jnp.maximum(first_max, second_max), axis=1)
    hidden_terms = hidden_terms + tie[0, 0]
    hidden_out = (middle_slot.astype(jnp.float32) + hidden_terms).astype(jnp.bfloat16)
    largest, hidden_out = lax.optimization_barrier((to_all(largest), hidden_out))
    max_logits = jnp.max(largest, axis=(0, 1))
    return (hidden_out, new_cache, last_norms, max_logits, head_input)


def solution(mesh):
    gx_count, gy_count = mesh.shape["gx"], mesh.shape["gy"]
    body = stationary if gx_count == KVH and gy_count == 4 else local
    in_specs = (
        P("gy", "gx"),
        P(),
        P("gy", "gx"),
        P("gx", "gy"),
        P(),
        P("gy", "gx"),
        P("gx", "gy"),
        P(),
        P(None, ("gx", "gy")),
        P(("gy", "gx"), None, None),
        P(),
        P(),
    )
    out_specs = (P("gy", "gx"), P(("gy", "gx"), None, None), P(), P(), P())
    return jax.shard_map(body, mesh=mesh, in_specs=in_specs, out_specs=out_specs, check_vma=False)
```
